256 devices in a mesh: inner: 8 (over x, core), outer: 16 (over z, y_hi), cfg: 2 (over y_lo).
Axes of the slice: x: 4, y: 4 (y_hi: 2, y_lo: 2; y = y_hi * 2 + y_lo), z: 8, core: 2. Of those that a mesh axis runs over, the one named last changes fastest.
Arguments:
- queries: bfloat16 [2, 8192, 2048], P('cfg', 'outer', 'inner'), may hold values from -6 to 6
- keys: bfloat16 [2, 8192, 2048], P('cfg', 'outer', 'inner'), may hold values from -6 to 6
- values: bfloat16 [2, 8192, 2048], P('cfg', 'outer', 'inner'), may hold values from -6 to 6
- outputs: bfloat16 [2, 8192, 2048], P('cfg', 'outer', 'inner'), may hold values from -8 to 8
- log_sums: float32 [2, 16, 8192], P('cfg', 'inner', 'outer'), may hold values from 9 to 10
- target: bfloat16 [8192, 2048], P('outer', 'inner'), may hold values from -6 to 6
Outputs:
- grad_queries: bfloat16 [2, 8192, 2048], P('cfg', 'outer', 'inner')
- grad_keys: bfloat16 [2, 8192, 2048], P('cfg', 'outer', 'inner')
- grad_values: bfloat16 [2, 8192, 2048], P('cfg', 'outer', 'inner')
The draws below stay inside these ranges and needn't reach their ends.
All inputs are finite; a program needn't handle non-finite values.
Results may differ from the reference program's by a relative error of at most 0.0059.
Values may be sent and summed in bfloat16 or wider, within the bound.
No kernel may reach another device: no remote copies, remote signals or barrier semaphores. Data moves between devices by JAX's collectives and lax.ppermute only.
A program may use at most 64 MiB of HBM per device.

```python
import math
import jax
import jax.numpy as jnp
from jax import lax

HEADS = 16
HEAD_DIM = 128
WIDTH = 2048
SEQ = 8192


def draw_outputs(key, part):
    key = jax.random.fold_in(key, 11)
    key_base, key_noise, key_rough, key_mixing = jax.random.split(key, 4)
    slope_power = 0.5
    basic_field = jax.random.normal(key_base, (SEQ, WIDTH), jnp.float32)
    noise_field = jax.random.normal(key_noise, (SEQ, WIDTH), jnp.float32)
    head_index = (jnp.arange(WIDTH) // HEAD_DIM).astype(jnp.float32)
    slope_scale = 3.0 ** (slope_power * head_index / (HEADS - 1))
    roughness = jax.random.uniform(key_rough, (WIDTH,), jnp.float32, 0.7, 1.4)
    feature_scale = slope_scale * roughness
    mixing = jax.random.uniform(key_mixing, (SEQ, 1), jnp.float32, 0.3, 1.5)
    unconditional = jnp.clip(basic_field * feature_scale, -8.0, 8.0)
    conditional = jnp.clip(mixing * unconditional + 0.25 * noise_field * feature_scale, -8.0, 8.0)
    return jnp.stack([conditional, unconditional]).astype(jnp.bfloat16)


def block_levels(stream_key, extent, pieces, smallest, largest):
    factor_of, own = 1.0, jax.random.fold_in(stream_key, 6)
    for dim, shards_of in pieces:
        heights = jnp.exp(jax.random.uniform(jax.random.fold_in(own, dim), (shards_of,), jnp.float32, smallest / len(pieces), largest / len(pieces)))
        factor_of = factor_of * jnp.repeat(heights, extent[dim] // shards_of).reshape([-1 if axis == dim else 1 for axis in range(len(extent))])
    return factor_of


def centred(own_key, extent, scale, bound, cuts=(), kind=jnp.bfloat16):
    result = jax.random.normal(own_key, extent, jnp.float32) * scale
    if len(cuts) > 0:
        result = block_levels(own_key, extent, cuts, -0.22, 0.18) * result
    return jnp.clip(result, min=-bound, max=bound).astype(kind)


def setup_inputs(seed: int = 0) -> dict:
    key_of = jax.random.split(jax.random.key(seed), 7)
    return {
        "queries": centred(key_of[0], (2, SEQ, WIDTH), 1.0, 6.0, ((0, 2), (1, 16), (2, 8))),
        "keys": centred(key_of[1], (2, SEQ, WIDTH), 1.0, 6.0, ((0, 2), (1, 16), (2, 8))),
        "values": centred(key_of[2], (2, SEQ, WIDTH), 1.0, 6.0, ((0, 2), (1, 16), (2, 8))),
        "outputs": draw_outputs(jax.random.fold_in(key_of[6], 71), 0),
        "log_sums": jnp.clip(9.0 + 1.0 * jax.random.uniform(key_of[4], (2, HEADS, SEQ), jnp.float32) ** block_levels(key_of[4], (2, HEADS, SEQ), ((0, 2), (1, 8), (2, 16)), -0.2, 0.2), 9.0, 10.0),
        "target": centred(key_of[5], (SEQ, WIDTH), 1.0, 6.0, ((0, 16), (1, 8))),
    }


guide_scale = 5.0
epsilon = 1e-6


def branch_grads(queries, keys, values, douts, log_sums, delta_sums):
    score_scale = HEAD_DIM ** -0.5
    length = queries.shape[0]
    query_heads = queries.astype(jnp.float32).reshape(length, HEADS, HEAD_DIM)
    key_heads = keys.astype(jnp.float32).reshape(length, HEADS, HEAD_DIM)
    value_heads = values.astype(jnp.float32).reshape(length, HEADS, HEAD_DIM)
    grad_heads = douts.astype(jnp.float32).reshape(length, HEADS, HEAD_DIM)
    block_rows = math.gcd(length, 512)
    block_count = length // block_rows

    def step(carry_pair, block_index):
        dk_total, dv_total = carry_pair
        block_start = (block_index * block_rows).astype(jnp.int32)
        query_block = lax.dynamic_slice_in_dim(query_heads, block_start, block_rows, 0)
        grad_block = lax.dynamic_slice_in_dim(grad_heads, block_start, block_rows, 0)
        log_block = lax.dynamic_slice_in_dim(log_sums, block_start, block_rows, 1)
        delta_block = lax.dynamic_slice_in_dim(delta_sums, block_start, block_rows, 1)
        scores = jnp.einsum("thd,shd->hts", query_block, key_heads) * score_scale
        weights = jnp.exp(scores - log_block[:, :, None])
        rounded = lax.optimization_barrier(weights.astype(jnp.bfloat16)).astype(jnp.float32)
        dv_term = jnp.einsum("hts,thd->shd", rounded, grad_block)
        dweights = jnp.einsum("thd,shd->hts", grad_block, value_heads)
        dscores = lax.optimization_barrier((weights * (dweights - delta_block[:, :, None])).astype(jnp.bfloat16)).astype(jnp.float32)
        dq_block = jnp.einsum("hts,shd->thd", dscores, key_heads) * score_scale
        dk_term = jnp.einsum("hts,thd->shd", dscores, query_block) * score_scale
        return (dk_total + dk_term, dv_total + dv_term), dq_block

    zero_heads = jnp.zeros((length, HEADS, HEAD_DIM), jnp.float32)
    (dk_total, dv_total), dq_blocks = lax.scan(step, (zero_heads, zero_heads), jnp.arange(block_count, dtype=jnp.int32))
    grad_q = dq_blocks.reshape(length, HEADS * HEAD_DIM).astype(jnp.bfloat16)
    grad_k = dk_total.reshape(length, HEADS * HEAD_DIM).astype(jnp.bfloat16)
    grad_v = dv_total.reshape(length, HEADS * HEAD_DIM).astype(jnp.bfloat16)
    return grad_q, grad_k, grad_v


def reference(queries, keys, values, outputs, log_sums, target):
    conditional = outputs[0].astype(jnp.float32)
    unconditional = outputs[1].astype(jnp.float32)
    denominator = jnp.sum(unconditional * unconditional, axis=-1, keepdims=True) + epsilon
    projection = jnp.sum(conditional * unconditional, axis=-1, keepdims=True) / denominator
    guided = projection * unconditional + guide_scale * (conditional - projection * unconditional)
    residual_term = guided - target.astype(jnp.float32)
    along_sum = jnp.sum(residual_term * unconditional, axis=-1, keepdims=True)
    grad_cond = guide_scale * residual_term + (1.0 - guide_scale) * along_sum * unconditional / denominator
    grad_uncond = (1.0 - guide_scale) * projection * residual_term + (1.0 - guide_scale) * along_sum * (conditional - 2.0 * projection * unconditional) / denominator
    douts = jnp.stack([grad_cond, grad_uncond]).astype(jnp.bfloat16)
    length = outputs.shape[1]
    products = douts.astype(jnp.float32).reshape(2, length, HEADS, HEAD_DIM) * outputs.astype(jnp.float32).reshape(2, length, HEADS, HEAD_DIM)
    delta_sums = jnp.transpose(jnp.sum(products, axis=-1), (0, 2, 1))
    first_grads = branch_grads(queries[0], keys[0], values[0], douts[0], log_sums[0], delta_sums[0])
    second_grads = branch_grads(queries[1], keys[1], values[1], douts[1], log_sums[1], delta_sums[1])
    grad_queries = jnp.stack([first_grads[0], second_grads[0]])
    grad_keys = jnp.stack([first_grads[1], second_grads[1]])
    grad_values = jnp.stack([first_grads[2], second_grads[2]])
    return grad_queries, grad_keys, grad_values
```

```python
import functools
import math

import jax
import jax.numpy as jnp
from jax import lax
from jax.experimental import pallas as pl
from jax.experimental.pallas import tpu as pltpu
from jax.sharding import Mesh, PartitionSpec as P

guide_scale = 5.0
epsilon = 1e-06
head_dim = 128
score_scale = head_dim**-0.5
log2e = math.log2(math.e)
extra_rows = 16

f32 = jnp.float32
bf16 = jnp.bfloat16
both_last = (((1,), (1,)), ((), ()))
whole = pl.BlockSpec(memory_space=pltpu.VMEM)


def params():
    return pltpu.CompilerParams(vmem_limit_bytes=40 * 1024 * 1024)


def split_rows(rows):
    length = rows.shape[1]
    lanes = jnp.concatenate(
        [
            jnp.concatenate([rows[h : h + 1, j : j + 128] for h in range(2)], axis=1)
            for j in range(0, length, 128)
        ],
        axis=0,
    )
    high = lanes.astype(bf16)
    rest = lanes - high.astype(f32)
    middle = rest.astype(bf16)
    low = (rest - middle.astype(f32)).astype(bf16)
    pad = jnp.zeros((extra_rows - 3 * lanes.shape[0], lanes.shape[1]), bf16)
    return jnp.concatenate([high, middle, low, pad], axis=0)


def joined_row(ref, tokens, lane):
    count = tokens // 128
    parts = ref[tokens : tokens + extra_rows, lane : lane + 128].astype(f32)
    rows = parts[:count] + parts[count : 2 * count] + parts[2 * count : 3 * count]
    return jnp.concatenate([rows[j : j + 1] for j in range(count)], axis=1)


def pack_queries_body(queries, log_sums, packed):
    tokens = queries.shape[0]
    packed[:tokens, :] = queries[...]
    packed[tokens:, :] = split_rows(log_sums[...] * log2e)


def pack_queries(queries, log_sums):
    tokens, width = queries.shape
    return pl.pallas_call(
        pack_queries_body,
        out_shape=jax.ShapeDtypeStruct((tokens + extra_rows, width), bf16),
        in_specs=[whole] * 2,
        out_specs=whole,
        compiler_params=params(),
    )(queries, log_sums)


def pack_keys_body(keys, values, packed):
    tokens = keys.shape[0]
    packed[:tokens, :] = keys[...]
    packed[tokens:, :] = values[...]


def pack_keys(keys, values):
    tokens, width = keys.shape
    return pl.pallas_call(
        pack_keys_body,
        out_shape=jax.ShapeDtypeStruct((2 * tokens, width), bf16),
        in_specs=[whole] * 2,
        out_specs=whole,
        compiler_params=params(),
    )(keys, values)


def columns_to_rows(columns):
    tokens = columns[0].shape[0]
    lane = lax.broadcasted_iota(jnp.int32, (tokens, 128), 1)
    table = jnp.zeros((tokens, 128), f32)
    for index, column in enumerate(columns):
        table = jnp.where(lane == index, column, table)
    return table.T[:8]


def fields(branch, own, far):
    own_field = own[...].astype(f32)
    far_field = far[...].astype(f32)
    first = branch[0] == 0
    return (
        own_field,
        jnp.where(first, own_field, far_field),
        jnp.where(first, far_field, own_field),
    )


def token_sums_body(branch, own, far, target, sums):
    _, cond, uncond = fields(branch, own, far)
    teacher = target[...].astype(f32)
    sums[...] = columns_to_rows(
        [
            jnp.sum(uncond * uncond, axis=1, keepdims=True),
            jnp.sum(cond * uncond, axis=1, keepdims=True),
            jnp.sum(teacher * uncond, axis=1, keepdims=True),
        ]
    )


def token_sums(branch, own, far, target):
    return pl.pallas_call(
        token_sums_body,
        out_shape=jax.ShapeDtypeStruct((8, own.shape[0]), f32),
        in_specs=[pl.BlockSpec(memory_space=pltpu.SMEM)] + [whole] * 3,
        out_specs=whole,
        compiler_params=params(),
    )(branch, own, far, target)


def output_grads_body(branch, own, far, target, sums_a, sums_b, sums_c, sums_d, packed):
    tokens = own.shape[0]
    own_field, cond, uncond = fields(branch, own, far)
    teacher = target[...].astype(f32)
    total = (sums_a[...] + sums_b[...]) + (sums_c[...] + sums_d[...])
    table = jnp.concatenate([total, jnp.zeros((120, tokens), f32)], axis=0).T
    square_sum = table[:, 0:1]
    cross_sum = table[:, 1:2]
    teacher_sum = table[:, 2:3]
    denominator = square_sum + epsilon
    projection = cross_sum / denominator
    projected = projection * uncond
    guided = projected + guide_scale * (cond - projected)
    residual = guided - teacher
    along = (
        guide_scale * cross_sum + (1.0 - guide_scale) * projection * square_sum - teacher_sum
    )
    pull = (1.0 - guide_scale) * along / denominator
    grad_cond = guide_scale * residual + pull * uncond
    grad_uncond = (1.0 - guide_scale) * projection * residual + pull * (cond - 2.0 * projected)
    douts = jnp.where(branch[0] == 0, grad_cond, grad_uncond).astype(bf16)
    packed[:tokens, :] = douts
    products = douts.astype(f32) * own_field
    deltas = columns_to_rows(
        [jnp.sum(products[:, h * 128 : h * 128 + 128], axis=1, keepdims=True) for h in range(2)]
    )
    packed[tokens:, :] = split_rows(deltas[:2])


def output_grads(branch, own, far, target, sums):
    tokens, width = own.shape
    return pl.pallas_call(
        output_grads_body,
        out_shape=jax.ShapeDtypeStruct((tokens + extra_rows, width), bf16),
        in_specs=[pl.BlockSpec(memory_space=pltpu.SMEM)] + [whole] * 7,
        out_specs=whole,
        compiler_params=params(),
    )(branch, own, far, target, *sums)


def attention_body(units, counts, first, last, *refs):
    takes = []
    for count in counts:
        takes.append(refs[:count])
        refs = refs[count:]
    queries, grads, blocks, turned = takes
    tokens = blocks[0].shape[0] // 2
    if not first:
        start_dk, start_dv = refs[:2]
        refs = refs[2:]
    dq_out, refs = refs[: len(units)], refs[len(units) :]
    if first:
        turned, refs = refs[-len(blocks) :], refs[: -len(blocks)]
        for both, across in zip(blocks, turned, strict=True):
            across[...] = both[:tokens, :].T
    if last:
        own_dk, own_dv, sent, dk_total, dv_total = refs
    else:
        dk_total, dv_total = refs
    seen = set()
    for unit, (query_at, query_lane, grad_at, grad_lane, head) in enumerate(units):
        feature = slice(head * 128, head * 128 + 128)
        query = queries[query_at][:tokens, query_lane : query_lane + 128]
        grad = grads[grad_at][:tokens, grad_lane : grad_lane + 128]
        log_row = joined_row(queries[query_at], tokens, query_lane)
        delta_row = joined_row(grads[grad_at], tokens, grad_lane)
        turned_dq = None
        for block, both in enumerate(blocks):
            rows = slice(block * tokens, block * tokens + tokens)
            key = both[:tokens, feature]
            value = both[tokens:, feature]
            scores = lax.dot_general(key, query, both_last, preferred_element_type=f32)
            weights = jnp.exp2(scores * (score_scale * log2e) - log_row)
            dweights = lax.dot_general(value, grad, both_last, preferred_element_type=f32)
            dscores = (weights * (dweights - delta_row)).astype(bf16)
            dv_term = jnp.dot(weights.astype(bf16), grad, preferred_element_type=f32)
            dk_term = jnp.dot(dscores, query, preferred_element_type=f32)
            if head in seen:
                dv_total[rows, feature] += dv_term
                dk_total[rows, feature] += dk_term
            elif first:
                dv_total[rows, feature] = dv_term
                dk_total[rows, feature] = dk_term
            else:
                dv_total[rows, feature] = start_dv[rows, feature] + dv_term
                dk_total[rows, feature] = start_dk[rows, feature] + dk_term
            term = jnp.dot(turned[block][feature, :], dscores, preferred_element_type=f32)
            turned_dq = term if turned_dq is None else turned_dq + term
        seen.add(head)
        dq_out[unit][...] = (turned_dq.T * score_scale).astype(dq_out[unit].dtype)
    if last:
        own_dk[...] = dk_total[:tokens, :] * score_scale
        own_dv[...] = dv_total[:tokens, :]
        sent[:tokens, :] = (dk_total[tokens:, :] * score_scale).astype(bf16)
        sent[tokens:, :] = dv_total[tokens:, :].astype(bf16)


def attention(units, queries, grads, blocks, turned, totals, out_types, last=False):
    tokens = blocks[0].shape[0] // 2
    first = totals is None
    groups = (queries, grads, blocks, turned)
    operands = [x for group in groups for x in group] + ([] if first else list(totals))
    rows = len(blocks) * tokens
    products = len(units) * 5 * tokens * rows * 128
    total_type = jax.ShapeDtypeStruct((rows, 256), f32)
    outs = [jax.ShapeDtypeStruct((tokens, 128), t) for t in out_types]
    if last:
        outs += [jax.ShapeDtypeStruct((tokens, 256), f32)] * 2
        outs += [jax.ShapeDtypeStruct((rows, 256), bf16)]
    else:
        outs += [total_type] * 2
    if first:
        outs += [jax.ShapeDtypeStruct((256, tokens), bf16)] * len(blocks)
    at = len(operands) - 2
    result = pl.pallas_call(
        functools.partial(attention_body, units, [len(g) for g in groups], first, last),
        out_shape=outs,
        in_specs=[whole] * len(operands),
        out_specs=[whole] * len(outs),
        scratch_shapes=[pltpu.VMEM(total_type.shape, f32)] * 2 if last else [],
        input_output_aliases=(
            {} if first or last else {at: len(units), at + 1: len(units) + 1}
        ),
        compiler_params=params(),
        cost_estimate=pl.CostEstimate(
            flops=4 * products, bytes_accessed=4 * 1024 * 1024, transcendentals=0
        ),
    )(*operands)
    return result[: len(units)], result[len(units) :]


def shift(x, by):
    peers = lax.axis_size("ring")
    return lax.ppermute(x, "ring", [(i, (i + by) % peers) for i in range(peers)])


def swap(x, axis):
    return lax.ppermute(x, axis, [(0, 1), (1, 0)])


def local(queries, keys, values, outputs, log_sums, target):
    tokens = keys.shape[1]
    own = outputs[0]
    far = swap(own, "cfg")
    query_block = pack_queries(queries[0], log_sums[0])
    branch = lax.axis_index("cfg").astype(jnp.int32).reshape(1)
    q1 = (shift(query_block, 1), shift(query_block, -1))
    sums = token_sums(branch, own, far, target)
    sums_core = swap(sums, "core")
    sums_core, q1 = lax.optimization_barrier((sums_core, q1))
    sums = sums + sums_core
    quads = [sums] + [
        lax.ppermute(sums, "x", [(i, (i + by) % 4) for i in range(4)]) for by in (1, 3, 2)
    ]
    q2 = (shift(q1[0], 1), shift(q1[1], -1))
    grad_block = output_grads(branch, own, far, target, quads)
    d1 = (shift(grad_block, 1), shift(grad_block, -1))
    own_keys, own_values, grad_block = lax.optimization_barrier(
        (keys[0], values[0], grad_block)
    )
    own_block = pack_keys(own_keys, own_values)
    far_block = swap(own_block, "pair")
    q3 = (shift(q2[0], 1), shift(q2[1], -1))
    d2 = (shift(d1[0], 1), shift(d1[1], -1))
    q4 = (shift(q3[0][:, :128], 1), shift(q3[1][:, 128:], -1))

    blocks = [own_block, far_block]
    own_units = ((0, 0, 0, 0, 0), (0, 128, 0, 128, 1))
    pair_units = own_units + ((1, 0, 1, 0, 0), (1, 128, 1, 128, 1))
    third_units = ((0, 0, 0, 0, 0), (0, 128, 2, 0, 1), (1, 0, 3, 0, 0), (1, 128, 1, 0, 1))
    last_units = ((0, 0, 0, 0, 0), (1, 0, 1, 0, 1))
    p0, totals = attention(
        own_units, (query_block,), (grad_block,), blocks, (), None, [f32] * 2
    )
    totals, turned = totals[:2], totals[2:]
    d2, q4, p0 = lax.optimization_barrier((d2, q4, p0))
    d3a = (shift(d2[0][:, :128], 1), shift(d2[1][:, 128:], -1))
    d3b = (shift(d2[0][:, 128:], 1), shift(d2[1][:, :128], -1))
    d4 = (shift(d3a[0], 1), shift(d3a[1], -1))

    run = functools.partial(attention, blocks=blocks, turned=turned)
    p3, totals = run(
        third_units, q3, d3a + d3b, totals=totals, out_types=[f32, bf16, bf16, f32]
    )
    p4, totals = run(last_units, q4, d4, totals=totals, out_types=[bf16] * 2)
    p2, totals = run(pair_units, q2, d2, totals=totals, out_types=[f32] * 4)
    p1, (dk_own, dv_own, sent) = run(
        pair_units, q1, d1, totals=totals, out_types=[f32] * 4, last=True
    )

    def joined(term, arrived):
        return (term + arrived.astype(f32)).astype(bf16)

    def home(right, left):
        return shift(right, -1), shift(left, 1)

    c_right, c_left = home(p3[1], p3[2])
    a_right, a_left = home(p4[0], p4[1])
    right, left = home(
        jnp.concatenate([joined(p3[0], a_right), joined(p2[1], c_right)], axis=1),
        jnp.concatenate([joined(p2[2], c_left), joined(p3[3], a_left)], axis=1),
    )
    right, left, sent = lax.optimization_barrier((right, left, sent))
    dkv_far = swap(sent, "pair")
    right, left = home(
        jnp.concatenate([joined(p2[0], right[:, :128]), joined(p1[1], right[:, 128:])], axis=1),
        jnp.concatenate([joined(p1[2], left[:, :128]), joined(p2[3], left[:, 128:])], axis=1),
    )
    a_right, a_left = home(joined(p1[0], right[:, :128]), joined(p1[3], left[:, 128:]))
    dq = [
        (p0[0] + a_right.astype(f32) + left[:, :128].astype(f32)).astype(bf16),
        (p0[1] + right[:, 128:].astype(f32) + a_left.astype(f32)).astype(bf16),
    ]
    grad_queries = jnp.concatenate(dq, axis=1)[None]
    grad_keys = (dk_own + dkv_far[:tokens].astype(f32)).astype(bf16)[None]
    grad_values = (dv_own + dkv_far[tokens:].astype(f32)).astype(bf16)[None]
    return (grad_queries, grad_keys, grad_values)


def solution(mesh):
    split = Mesh(
        mesh.devices.reshape(4, 2, 8, 2, 2), ("x", "core", "ring", "pair", "cfg")
    )
    rows, columns = ("ring", "pair"), ("x", "core")
    in_specs = (
        P("cfg", rows, columns),
        P("cfg", rows, columns),
        P("cfg", rows, columns),
        P("cfg", rows, columns),
        P("cfg", columns, rows),
        P(rows, columns),
    )
    out_specs = (P("cfg", rows, columns),) * 3
    return jax.shard_map(
        local, mesh=split, in_specs=in_specs, out_specs=out_specs, check_vma=False
    )
```

```python
import functools
import math

import jax
import jax.numpy as jnp
from jax import lax
from jax.experimental import pallas as pl
from jax.experimental.pallas import tpu as pltpu
from jax.sharding import Mesh, PartitionSpec as P

guide_scale = 5.0
epsilon = 1e-06
head_dim = 128
score_scale = head_dim**-0.5
log2e = math.log2(math.e)
extra_rows = 16

f32 = jnp.float32
bf16 = jnp.bfloat16
both_last = (((1,), (1,)), ((), ()))
whole = pl.BlockSpec(memory_space=pltpu.VMEM)


def params():
    return pltpu.CompilerParams(vmem_limit_bytes=40 * 1024 * 1024)


def split_rows(rows):
    length = rows.shape[1]
    lanes = jnp.concatenate(
        [
            jnp.concatenate([rows[h : h + 1, j : j + 128] for h in range(2)], axis=1)
            for j in range(0, length, 128)
        ],
        axis=0,
    )
    high = lanes.astype(bf16)
    rest = lanes - high.astype(f32)
    middle = rest.astype(bf16)
    low = (rest - middle.astype(f32)).astype(bf16)
    pad = jnp.zeros((extra_rows - 3 * lanes.shape[0], lanes.shape[1]), bf16)
    return jnp.concatenate([high, middle, low, pad], axis=0)


def joined_row(ref, tokens, lane):
    count = tokens // 128
    parts = ref[tokens : tokens + extra_rows, lane : lane + 128].astype(f32)
    rows = parts[:count] + parts[count : 2 * count] + parts[2 * count : 3 * count]
    return jnp.concatenate([rows[j : j + 1] for j in range(count)], axis=1)


def pack_queries_body(queries, log_sums, packed):
    tokens = queries.shape[0]
    packed[:tokens, :] = queries[...]
    packed[tokens:, :] = split_rows(log_sums[...] * log2e)


def pack_queries(queries, log_sums):
    tokens, width = queries.shape
    return pl.pallas_call(
        pack_queries_body,
        out_shape=jax.ShapeDtypeStruct((tokens + extra_rows, width), bf16),
        in_specs=[whole] * 2,
        out_specs=whole,
        compiler_params=params(),
    )(queries, log_sums)


def pack_keys_body(keys, values, packed, turned):
    tokens = keys.shape[0]
    packed[:tokens, :] = keys[...]
    packed[tokens:, :] = values[...]
    turned[...] = keys[...].T


def pack_keys(keys, values):
    tokens, width = keys.shape
    return pl.pallas_call(
        pack_keys_body,
        out_shape=[
            jax.ShapeDtypeStruct((2 * tokens, width), bf16),
            jax.ShapeDtypeStruct((width, tokens), bf16),
        ],
        in_specs=[whole] * 2,
        out_specs=[whole] * 2,
        compiler_params=params(),
    )(keys, values)


def columns_to_rows(columns):
    tokens = columns[0].shape[0]
    lane = lax.broadcasted_iota(jnp.int32, (tokens, 128), 1)
    table = jnp.zeros((tokens, 128), f32)
    for index, column in enumerate(columns):
        table = jnp.where(lane == index, column, table)
    return table.T[:8]


def fields(branch, own, far):
    own_field = own[...].astype(f32)
    far_field = far[...].astype(f32)
    first = branch[0] == 0
    return (
        own_field,
        jnp.where(first, own_field, far_field),
        jnp.where(first, far_field, own_field),
    )


def token_sums_body(branch, own, far, target, sums):
    _, cond, uncond = fields(branch, own, far)
    teacher = target[...].astype(f32)
    sums[...] = columns_to_rows(
        [
            jnp.sum(uncond * uncond, axis=1, keepdims=True),
            jnp.sum(cond * uncond, axis=1, keepdims=True),
            jnp.sum(teacher * uncond, axis=1, keepdims=True),
        ]
    )


def token_sums(branch, own, far, target):
    return pl.pallas_call(
        token_sums_body,
        out_shape=jax.ShapeDtypeStruct((8, own.shape[0]), f32),
        in_specs=[pl.BlockSpec(memory_space=pltpu.SMEM)] + [whole] * 3,
        out_specs=whole,
        compiler_params=params(),
    )(branch, own, far, target)


def output_grads_body(branch, own, far, target, sums_a, sums_b, packed):
    tokens = own.shape[0]
    own_field, cond, uncond = fields(branch, own, far)
    teacher = target[...].astype(f32)
    total = sums_a[...] + sums_b[...]
    table = jnp.concatenate([total, jnp.zeros((120, tokens), f32)], axis=0).T
    square_sum = table[:, 0:1]
    cross_sum = table[:, 1:2]
    teacher_sum = table[:, 2:3]
    denominator = square_sum + epsilon
    projection = cross_sum / denominator
    projected = projection * uncond
    guided = projected + guide_scale * (cond - projected)
    residual = guided - teacher
    along = (
        guide_scale * cross_sum + (1.0 - guide_scale) * projection * square_sum - teacher_sum
    )
    pull = (1.0 - guide_scale) * along / denominator
    grad_cond = guide_scale * residual + pull * uncond
    grad_uncond = (1.0 - guide_scale) * projection * residual + pull * (cond - 2.0 * projected)
    douts = jnp.where(branch[0] == 0, grad_cond, grad_uncond).astype(bf16)
    packed[:tokens, :] = douts
    products = douts.astype(f32) * own_field
    deltas = columns_to_rows(
        [jnp.sum(products[:, h * 128 : h * 128 + 128], axis=1, keepdims=True) for h in range(2)]
    )
    packed[tokens:, :] = split_rows(deltas[:2])


def output_grads(branch, own, far, target, sums):
    tokens, width = own.shape
    return pl.pallas_call(
        output_grads_body,
        out_shape=jax.ShapeDtypeStruct((tokens + extra_rows, width), bf16),
        in_specs=[pl.BlockSpec(memory_space=pltpu.SMEM)] + [whole] * 5,
        out_specs=whole,
        compiler_params=params(),
    )(branch, own, far, target, *sums)


def attention_body(units, counts, modes, *refs):
    turn, started, ends, partial = modes
    takes = []
    for count in counts:
        takes.append(refs[:count])
        refs = refs[count:]
    queries, grads, blocks, turned, starts, terms = takes
    tokens = blocks[0].shape[0] // 2
    dq_out, refs = refs[: len(units)], refs[len(units) :]
    if turn:
        turned, refs = refs[: len(blocks)], refs[len(blocks) :]
        for both, across in zip(blocks, turned, strict=True):
            across[...] = both[:tokens, :].T
    scratch = list(refs[len(blocks) :])
    results = refs[: len(blocks)]
    totals = [r if end is None else scratch.pop(0) for r, end in zip(results, ends, strict=True)]
    seen = set()
    for unit, (query_at, query_lane, grad_at, grad_lane, head) in enumerate(units):
        feature = slice(head * 128, head * 128 + 128)
        query = queries[query_at][:tokens, query_lane : query_lane + 128]
        grad = grads[grad_at][:tokens, grad_lane : grad_lane + 128]
        log_row = joined_row(queries[query_at], tokens, query_lane)
        delta_row = joined_row(grads[grad_at], tokens, grad_lane)
        turned_dq = None
        for block, both in enumerate(blocks):
            total = totals[block]
            key = both[:tokens, feature]
            value = both[tokens:, feature]
            scores = lax.dot_general(key, query, both_last, preferred_element_type=f32)
            weights = jnp.exp2(scores * (score_scale * log2e) - log_row)
            dweights = lax.dot_general(value, grad, both_last, preferred_element_type=f32)
            dscores = (weights * (dweights - delta_row)).astype(bf16)
            dv_term = jnp.dot(weights.astype(bf16), grad, preferred_element_type=f32)
            dk_term = jnp.dot(dscores, query, preferred_element_type=f32)
            if head in seen:
                total[tokens:, feature] += dv_term
                total[:tokens, feature] += dk_term
            elif started:
                total[tokens:, feature] = starts[block][tokens:, feature] + dv_term
                total[:tokens, feature] = starts[block][:tokens, feature] + dk_term
            else:
                total[tokens:, feature] = dv_term
                total[:tokens, feature] = dk_term
            term = jnp.dot(turned[block][feature, :], dscores, preferred_element_type=f32)
            turned_dq = term if turned_dq is None else turned_dq + term
        seen.add(head)
        dq = turned_dq.T * score_scale
        if partial:
            dq = dq + terms[unit][...]
        dq_out[unit][...] = dq.astype(dq_out[unit].dtype)
    for done, total, end in zip(results, totals, ends, strict=True):
        if end is not None:
            done[:tokens, :] = (total[:tokens, :] * score_scale).astype(end)
            done[tokens:, :] = total[tokens:, :].astype(end)


def attention(units, queries, grads, blocks, turned, totals, out_types, ends=None, terms=()):
    tokens = blocks[0].shape[0] // 2
    groups = (queries, grads, blocks, turned, totals, terms)
    operands = [x for group in groups for x in group]
    ends = ends or [None] * len(blocks)
    turn = not turned
    outs = [jax.ShapeDtypeStruct((tokens, 128), t) for t in out_types]
    if turn:
        outs += [jax.ShapeDtypeStruct((256, tokens), bf16)] * len(blocks)
    at = len(operands) - len(terms) - len(totals)
    aliases = {
        at + i: len(outs) + i for i in range(len(totals)) if ends[i] is None
    }
    outs += [jax.ShapeDtypeStruct((2 * tokens, 256), end or f32) for end in ends]
    scratch = [pltpu.VMEM((2 * tokens, 256), f32) for end in ends if end is not None]
    products = len(units) * 5 * tokens * len(blocks) * tokens * 128
    result = pl.pallas_call(
        functools.partial(
            attention_body,
            units,
            [len(g) for g in groups],
            (turn, bool(totals), ends, bool(terms)),
        ),
        out_shape=outs,
        in_specs=[whole] * len(operands),
        out_specs=[whole] * len(outs),
        scratch_shapes=scratch,
        input_output_aliases=aliases,
        compiler_params=params(),
        cost_estimate=pl.CostEstimate(
            flops=4 * products, bytes_accessed=4 * 1024 * 1024, transcendentals=0
        ),
    )(*operands)
    return result[: len(units)], result[len(units) :]


def shift(x, by):
    peers = lax.axis_size("ring")
    return lax.ppermute(x, "ring", [(i, (i + by) % peers) for i in range(peers)])


def swap(x, axis):
    return lax.ppermute(x, axis, [(0, 1), (1, 0)])


def local(queries, keys, values, outputs, log_sums, target):
    tokens = keys.shape[1]
    own = outputs[0]
    far = swap(own, "cfg")
    query_block = pack_queries(queries[0], log_sums[0])
    branch = lax.axis_index("cfg").astype(jnp.int32).reshape(1)
    query_block, own_keys, own_values = lax.optimization_barrier(
        (query_block, keys[0], values[0])
    )
    own_block, own_turned = pack_keys(own_keys, own_values)
    far_block = swap(own_block, "pair")
    q1 = (shift(query_block, 1), shift(query_block, -1))
    sums = token_sums(branch, own, far, target)
    sums = sums + swap(sums, "core")
    sums_near = lax.ppermute(sums, "x", [(i, i ^ 1) for i in range(4)])
    sums_near, q1 = lax.optimization_barrier((sums_near, q1))
    sums = sums + sums_near
    sums_far = lax.ppermute(sums, "x", [(i, 3 - i) for i in range(4)])
    q2 = (shift(q1[0], 1), shift(q1[1], -1))
    grad_block = output_grads(branch, own, far, target, [sums, sums_far])
    d1 = (shift(grad_block, 1), shift(grad_block, -1))
    q3 = (shift(q2[0], 1), shift(q2[1], -1))
    d2 = (shift(d1[0], 1), shift(d1[1], -1))
    q4 = (shift(q3[0][:, :128], 1), shift(q3[1][:, 128:], -1))

    blocks = [own_block, far_block]
    pair_units = (
        (0, 0, 0, 0, 0),
        (0, 128, 0, 128, 1),
        (1, 0, 1, 0, 0),
        (1, 128, 1, 128, 1),
    )
    near_units = pair_units + ((2, 0, 2, 0, 0), (2, 128, 2, 128, 1))
    last_units = ((0, 0, 0, 0, 0), (1, 0, 1, 0, 1))
    near = (near_units, (*q1, query_block), (*d1, grad_block))
    near_terms, (far_turned, far_total) = attention(*near, blocks[1:], (), (), [f32] * 6)
    d2, q4, near_terms = lax.optimization_barrier((d2, q4, near_terms))
    d4 = (shift(d2[0][:, :128], 2), shift(d2[1][:, 128:], -2))
    d3 = (shift(d2[0], 1), shift(d2[1], -1))
    run = functools.partial(attention, blocks=blocks, turned=(own_turned, far_turned))
    zeros = jnp.zeros_like(far_total)
    p3, totals = run(
        pair_units, q3, d3, totals=(zeros, far_total), out_types=[bf16] * 4
    )
    p4, totals = run(last_units, q4, d4, totals=totals, out_types=[bf16] * 2)
    p2, (own_total, sent) = run(
        pair_units, q2, d2, totals=totals, out_types=[f32] * 4, ends=[None, bf16]
    )

    def home(right, left, steps=1):
        return lax.optimization_barrier((shift(right, -steps), shift(left, steps)))

    def beside(first, second):
        return jnp.concatenate([first, second], axis=1)

    def joined(first, second, arrived):
        return (beside(first, second) + arrived.astype(f32)).astype(bf16)

    a_right, a_left = home(*p4, steps=2)
    right, left = home(beside(p3[0], p3[1]), beside(p3[2], p3[3]))
    right, left, sent = lax.optimization_barrier((right, left, sent))
    dkv_far = swap(sent, "pair")
    right = joined(p2[0] + a_right.astype(f32), p2[1], right)
    left = joined(p2[2], p2[3] + a_left.astype(f32), left)
    right, left = home(right, left)
    near_terms, (dkv_own,) = attention(
        *near, blocks[:1], (own_turned,), (own_total,), [f32] * 6, ends=[f32], terms=near_terms
    )
    p1, p0 = near_terms[:4], near_terms[4:]
    right, left = home(joined(p1[0], p1[1], right), joined(p1[2], p1[3], left))
    dq = beside(*p0) + right.astype(f32) + left.astype(f32)
    grad_queries = dq.astype(bf16)[None]
    dkv = (dkv_own + dkv_far.astype(f32)).astype(bf16)
    return (grad_queries, dkv[:tokens][None], dkv[tokens:][None])


def solution(mesh):
    split = Mesh(
        mesh.devices.reshape(4, 2, 8, 2, 2), ("x", "core", "ring", "pair", "cfg")
    )
    rows, columns = ("ring", "pair"), ("x", "core")
    in_specs = (
        P("cfg", rows, columns),
        P("cfg", rows, columns),
        P("cfg", rows, columns),
        P("cfg", rows, columns),
        P("cfg", columns, rows),
        P(rows, columns),
    )
    out_specs = (P("cfg", rows, columns),) * 3
    return jax.shard_map(
        local, mesh=split, in_specs=in_specs, out_specs=out_specs, check_vma=False
    )
```

```python
import functools
import math

import jax
import jax.numpy as jnp
from jax import lax
from jax.experimental import pallas as pl
from jax.experimental.pallas import tpu as pltpu
from jax.sharding import Mesh, PartitionSpec as P

guide_scale = 5.0
epsilon = 1e-06
head_dim = 128
score_scale = head_dim**-0.5
log2e = math.log2(math.e)
extra_rows = 16

f32 = jnp.float32
bf16 = jnp.bfloat16
both_last = (((1,), (1,)), ((), ()))
whole = pl.BlockSpec(memory_space=pltpu.VMEM)


def params():
    return pltpu.CompilerParams(vmem_limit_bytes=40 * 1024 * 1024)


def split_rows(rows):
    length = rows.shape[1]
    lanes = jnp.concatenate(
        [
            jnp.concatenate([rows[h : h + 1, j : j + 128] for h in range(2)], axis=1)
            for j in range(0, length, 128)
        ],
        axis=0,
    )
    high = lanes.astype(bf16)
    rest = lanes - high.astype(f32)
    middle = rest.astype(bf16)
    low = (rest - middle.astype(f32)).astype(bf16)
    pad = jnp.zeros((extra_rows - 3 * lanes.shape[0], lanes.shape[1]), bf16)
    return jnp.concatenate([high, middle, low, pad], axis=0)


def joined_row(ref, tokens, lane):
    count = tokens // 128
    parts = ref[tokens : tokens + extra_rows, lane : lane + 128].astype(f32)
    rows = parts[:count] + parts[count : 2 * count] + parts[2 * count : 3 * count]
    return jnp.concatenate([rows[j : j + 1] for j in range(count)], axis=1)


def pack_queries_body(queries, log_sums, packed):
    tokens = queries.shape[0]
    packed[:tokens, :] = queries[...]
    packed[tokens:, :] = split_rows(log_sums[...] * log2e)


def pack_queries(queries, log_sums):
    tokens, width = queries.shape
    return pl.pallas_call(
        pack_queries_body,
        out_shape=jax.ShapeDtypeStruct((tokens + extra_rows, width), bf16),
        in_specs=[whole] * 2,
        out_specs=whole,
        compiler_params=params(),
    )(queries, log_sums)


def pack_keys_body(keys, values, packed, turned):
    tokens = keys.shape[0]
    packed[:tokens, :] = keys[...]
    packed[tokens:, :] = values[...]
    turned[...] = keys[...].T


def pack_keys(keys, values):
    tokens, width = keys.shape
    return pl.pallas_call(
        pack_keys_body,
        out_shape=[
            jax.ShapeDtypeStruct((2 * tokens, width), bf16),
            jax.ShapeDtypeStruct((width, tokens), bf16),
        ],
        in_specs=[whole] * 2,
        out_specs=[whole] * 2,
        compiler_params=params(),
    )(keys, values)


def columns_to_rows(columns):
    tokens = columns[0].shape[0]
    lane = lax.broadcasted_iota(jnp.int32, (tokens, 128), 1)
    table = jnp.zeros((tokens, 128), f32)
    for index, column in enumerate(columns):
        table = jnp.where(lane == index, column, table)
    return table.T[:8]


def fields(branch, own, far):
    own_field = own[...].astype(f32)
    far_field = far[...].astype(f32)
    first = branch[0] == 0
    return (
        own_field,
        jnp.where(first, own_field, far_field),
        jnp.where(first, far_field, own_field),
    )


def token_sums_body(branch, own, far, target, sums):
    _, cond, uncond = fields(branch, own, far)
    teacher = target[...].astype(f32)
    sums[...] = columns_to_rows(
        [
            jnp.sum(uncond * uncond, axis=1, keepdims=True),
            jnp.sum(cond * uncond, axis=1, keepdims=True),
            jnp.sum(teacher * uncond, axis=1, keepdims=True),
        ]
    )


def token_sums(branch, own, far, target):
    return pl.pallas_call(
        token_sums_body,
        out_shape=jax.ShapeDtypeStruct((8, own.shape[0]), f32),
        in_specs=[pl.BlockSpec(memory_space=pltpu.SMEM)] + [whole] * 3,
        out_specs=whole,
        compiler_params=params(),
    )(branch, own, far, target)


def output_grads_body(branch, own, far, target, sums_a, sums_b, packed):
    tokens = own.shape[0]
    own_field, cond, uncond = fields(branch, own, far)
    teacher = target[...].astype(f32)
    total = sums_a[...] + sums_b[...]
    table = jnp.concatenate([total, jnp.zeros((120, tokens), f32)], axis=0).T
    square_sum = table[:, 0:1]
    cross_sum = table[:, 1:2]
    teacher_sum = table[:, 2:3]
    denominator = square_sum + epsilon
    projection = cross_sum / denominator
    projected = projection * uncond
    guided = projected + guide_scale * (cond - projected)
    residual = guided - teacher
    along = (
        guide_scale * cross_sum + (1.0 - guide_scale) * projection * square_sum - teacher_sum
    )
    pull = (1.0 - guide_scale) * along / denominator
    grad_cond = guide_scale * residual + pull * uncond
    grad_uncond = (1.0 - guide_scale) * projection * residual + pull * (cond - 2.0 * projected)
    douts = jnp.where(branch[0] == 0, grad_cond, grad_uncond).astype(bf16)
    packed[:tokens, :] = douts
    products = douts.astype(f32) * own_field
    deltas = columns_to_rows(
        [jnp.sum(products[:, h * 128 : h * 128 + 128], axis=1, keepdims=True) for h in range(2)]
    )
    packed[tokens:, :] = split_rows(deltas[:2])


def output_grads(branch, own, far, target, sums):
    tokens, width = own.shape
    return pl.pallas_call(
        output_grads_body,
        out_shape=jax.ShapeDtypeStruct((tokens + extra_rows, width), bf16),
        in_specs=[pl.BlockSpec(memory_space=pltpu.SMEM)] + [whole] * 5,
        out_specs=whole,
        compiler_params=params(),
    )(branch, own, far, target, *sums)


def attention_body(units, counts, modes, *refs):
    turn, started, ends, partial = modes
    takes = []
    for count in counts:
        takes.append(refs[:count])
        refs = refs[count:]
    queries, grads, blocks, turned, starts, terms = takes
    tokens = blocks[0].shape[0] // 2
    dq_out, refs = refs[: len(units)], refs[len(units) :]
    if turn:
        turned, refs = refs[: len(blocks)], refs[len(blocks) :]
        for both, across in zip(blocks, turned, strict=True):
            across[...] = both[:tokens, :].T
    scratch = list(refs[len(blocks) :])
    results = refs[: len(blocks)]
    totals = [r if end is None else scratch.pop(0) for r, end in zip(results, ends, strict=True)]
    seen = set()
    for unit, (query_at, query_lane, grad_at, grad_lane, head) in enumerate(units):
        feature = slice(head * 128, head * 128 + 128)
        query = queries[query_at][:tokens, query_lane : query_lane + 128]
        grad = grads[grad_at][:tokens, grad_lane : grad_lane + 128]
        log_row = joined_row(queries[query_at], tokens, query_lane)
        delta_row = joined_row(grads[grad_at], tokens, grad_lane)
        turned_dq = None
        for block, both in enumerate(blocks):
            total = totals[block]
            key = both[:tokens, feature]
            value = both[tokens:, feature]
            scores = lax.dot_general(key, query, both_last, preferred_element_type=f32)
            weights = jnp.exp2(scores * (score_scale * log2e) - log_row)
            dweights = lax.dot_general(value, grad, both_last, preferred_element_type=f32)
            dscores = (weights * (dweights - delta_row)).astype(bf16)
            dv_term = jnp.dot(weights.astype(bf16), grad, preferred_element_type=f32)
            dk_term = jnp.dot(dscores, query, preferred_element_type=f32)
            if head in seen:
                total[tokens:, feature] += dv_term
                total[:tokens, feature] += dk_term
            elif started:
                total[tokens:, feature] = starts[block][tokens:, feature] + dv_term
                total[:tokens, feature] = starts[block][:tokens, feature] + dk_term
            else:
                total[tokens:, feature] = dv_term
                total[:tokens, feature] = dk_term
            term = jnp.dot(turned[block][feature, :], dscores, preferred_element_type=f32)
            turned_dq = term if turned_dq is None else turned_dq + term
        seen.add(head)
        dq = turned_dq.T * score_scale
        if partial:
            dq = dq + terms[unit][...]
        dq_out[unit][...] = dq.astype(dq_out[unit].dtype)
    for done, total, end in zip(results, totals, ends, strict=True):
        if end is not None:
            done[:tokens, :] = (total[:tokens, :] * score_scale).astype(end)
            done[tokens:, :] = total[tokens:, :].astype(end)


def attention(units, queries, grads, blocks, turned, totals, out_types, ends=None, terms=()):
    tokens = blocks[0].shape[0] // 2
    groups = (queries, grads, blocks, turned, totals, terms)
    operands = [x for group in groups for x in group]
    ends = ends or [None] * len(blocks)
    turn = not turned
    outs = [jax.ShapeDtypeStruct((tokens, 128), t) for t in out_types]
    if turn:
        outs += [jax.ShapeDtypeStruct((256, tokens), bf16)] * len(blocks)
    at = len(operands) - len(terms) - len(totals)
    aliases = {
        at + i: len(outs) + i for i in range(len(totals)) if ends[i] is None
    }
    outs += [jax.ShapeDtypeStruct((2 * tokens, 256), end or f32) for end in ends]
    scratch = [pltpu.VMEM((2 * tokens, 256), f32) for end in ends if end is not None]
    products = len(units) * 5 * tokens * len(blocks) * tokens * 128
    result = pl.pallas_call(
        functools.partial(
            attention_body,
            units,
            [len(g) for g in groups],
            (turn, bool(totals), ends, bool(terms)),
        ),
        out_shape=outs,
        in_specs=[whole] * len(operands),
        out_specs=[whole] * len(outs),
        scratch_shapes=scratch,
        input_output_aliases=aliases,
        compiler_params=params(),
        cost_estimate=pl.CostEstimate(
            flops=4 * products, bytes_accessed=4 * 1024 * 1024, transcendentals=0
        ),
    )(*operands)
    return result[: len(units)], result[len(units) :]


def shift(x, by):
    peers = lax.axis_size("ring")
    return lax.ppermute(x, "ring", [(i, (i + by) % peers) for i in range(peers)])


def swap(x, axis):
    return lax.ppermute(x, axis, [(0, 1), (1, 0)])


def local(queries, keys, values, outputs, log_sums, target):
    tokens = keys.shape[1]
    own = outputs[0]
    far = swap(own, "cfg")
    query_block = pack_queries(queries[0], log_sums[0])
    branch = lax.axis_index("cfg").astype(jnp.int32).reshape(1)
    query_block, own_keys, own_values = lax.optimization_barrier(
        (query_block, keys[0], values[0])
    )
    own_block, own_turned = pack_keys(own_keys, own_values)
    far_block = swap(own_block, "pair")
    q1 = (shift(query_block, 1), shift(query_block, -1))
    sums = token_sums(branch, own, far, target)
    sums = sums + swap(sums, "core")
    sums_near = lax.ppermute(sums, "x", [(i, i ^ 1) for i in range(4)])
    sums_near, q1 = lax.optimization_barrier((sums_near, q1))
    sums = sums + sums_near
    sums_far = lax.ppermute(sums, "x", [(i, 3 - i) for i in range(4)])
    q2 = (shift(q1[0], 1), shift(q1[1], -1))
    grad_block = output_grads(branch, own, far, target, [sums, sums_far])
    d1 = (shift(grad_block, 1), shift(grad_block, -1))
    q3 = (shift(q2[0], 1), shift(q2[1], -1))
    d2 = (shift(d1[0], 1), shift(d1[1], -1))

    blocks = [own_block, far_block]
    pair_units = (
        (0, 0, 0, 0, 0),
        (0, 128, 0, 128, 1),
        (1, 0, 1, 0, 0),
        (1, 128, 1, 128, 1),
    )
    near_units = pair_units + ((2, 0, 2, 0, 0), (2, 128, 2, 128, 1))
    last_units = ((0, 256, 0, 0, 0), (1, 256, 1, 0, 1))
    near = (near_units, (*q1, query_block), (*d1, grad_block))
    near_terms, (far_turned, far_total) = attention(*near, blocks[1:], (), (), [f32] * 6)
    d2, near_terms = lax.optimization_barrier((d2, near_terms))
    ahead = (
        jnp.concatenate([d2[0], q3[0][:, :128]], axis=1),
        jnp.concatenate([d2[1], q3[1][:, 128:]], axis=1),
    )
    d3 = (shift(ahead[0], 1), shift(ahead[1], -1))
    d4 = (shift(d3[0][:, :128], 1), shift(d3[1][:, 128:256], -1))
    run = functools.partial(attention, blocks=blocks, turned=(own_turned, far_turned))
    p1, (own_total,) = attention(
        pair_units, q1, d1, blocks[:1], (own_turned,), (), [f32] * 4, terms=near_terms[:4]
    )
    p3, totals = run(
        pair_units, q3, d3, totals=(own_total, far_total), out_types=[bf16] * 4
    )
    p4, totals = run(last_units, d3, d4, totals=totals, out_types=[bf16] * 2)
    p2, (own_total, sent) = run(
        pair_units, q2, d2, totals=totals, out_types=[f32] * 4, ends=[None, bf16]
    )

    def home(right, left, steps=1):
        return lax.optimization_barrier((shift(right, -steps), shift(left, steps)))

    def beside(first, second):
        return jnp.concatenate([first, second], axis=1)

    def joined(first, second, arrived):
        return (beside(first, second) + arrived.astype(f32)).astype(bf16)

    a_right, a_left = home(*p4, steps=2)
    right, left = home(beside(p3[0], p3[1]), beside(p3[2], p3[3]))
    right, left, own_total = lax.optimization_barrier((right, left, own_total))
    right = joined(p2[0] + a_right.astype(f32), p2[1], right)
    left = joined(p2[2], p2[3] + a_left.astype(f32), left)
    right, left = home(right, left)
    p0, (dkv_own,) = attention(
        pair_units[:2],
        (query_block,),
        (grad_block,),
        blocks[:1],
        (own_turned,),
        (own_total,),
        [f32] * 2,
        ends=[f32],
        terms=near_terms[4:],
    )
    p0, sent = lax.optimization_barrier((p0, sent))
    dkv_far = swap(sent, "pair")
    right, left = home(joined(p1[0], p1[1], right), joined(p1[2], p1[3], left))
    dq = beside(*p0) + right.astype(f32) + left.astype(f32)
    grad_queries = dq.astype(bf16)[None]
    dkv = (dkv_own + dkv_far.astype(f32)).astype(bf16)
    return (grad_queries, dkv[:tokens][None], dkv[tokens:][None])


def solution(mesh):
    split = Mesh(
        mesh.devices.reshape(4, 2, 8, 2, 2), ("x", "core", "ring", "pair", "cfg")
    )
    rows, columns = ("ring", "pair"), ("x", "core")
    in_specs = (
        P("cfg", rows, columns),
        P("cfg", rows, columns),
        P("cfg", rows, columns),
        P("cfg", rows, columns),
        P("cfg", columns, rows),
        P(rows, columns),
    )
    out_specs = (P("cfg", rows, columns),) * 3
    return jax.shard_map(
        local, mesh=split, in_specs=in_specs, out_specs=out_specs, check_vma=False
    )
```

```python
import functools
import math

import jax
import jax.numpy as jnp
from jax import lax
from jax.experimental import pallas as pl
from jax.experimental.pallas import tpu as pltpu
from jax.sharding import Mesh, PartitionSpec as P

guide_scale = 5.0
epsilon = 1e-06
head_dim = 128
score_scale = head_dim**-0.5
log2e = math.log2(math.e)
extra_rows = 16

f32 = jnp.float32
bf16 = jnp.bfloat16
both_last = (((1,), (1,)), ((), ()))
whole = pl.BlockSpec(memory_space=pltpu.VMEM)


def params():
    return pltpu.CompilerParams(vmem_limit_bytes=40 * 1024 * 1024)


def split_rows(rows):
    length = rows.shape[1]
    lanes = jnp.concatenate(
        [
            jnp.concatenate([rows[h : h + 1, j : j + 128] for h in range(2)], axis=1)
            for j in range(0, length, 128)
        ],
        axis=0,
    )
    high = lanes.astype(bf16)
    rest = lanes - high.astype(f32)
    middle = rest.astype(bf16)
    low = (rest - middle.astype(f32)).astype(bf16)
    pad = jnp.zeros((extra_rows - 3 * lanes.shape[0], lanes.shape[1]), bf16)
    return jnp.concatenate([high, middle, low, pad], axis=0)


def joined_row(ref, tokens, lane):
    count = tokens // 128
    parts = ref[tokens : tokens + extra_rows, lane : lane + 128].astype(f32)
    rows = parts[:count] + parts[count : 2 * count] + parts[2 * count : 3 * count]
    return jnp.concatenate([rows[j : j + 1] for j in range(count)], axis=1)


def pack_queries_body(queries, log_sums, packed):
    tokens = queries.shape[0]
    packed[:tokens, :] = queries[...]
    packed[tokens:, :] = split_rows(log_sums[...] * log2e)


def pack_queries(queries, log_sums):
    tokens, width = queries.shape
    return pl.pallas_call(
        pack_queries_body,
        out_shape=jax.ShapeDtypeStruct((tokens + extra_rows, width), bf16),
        in_specs=[whole] * 2,
        out_specs=whole,
        compiler_params=params(),
    )(queries, log_sums)


def pack_keys_body(keys, values, packed, turned):
    tokens = keys.shape[0]
    packed[:tokens, :] = keys[...]
    packed[tokens:, :] = values[...]
    turned[...] = keys[...].T


def pack_keys(keys, values):
    tokens, width = keys.shape
    return pl.pallas_call(
        pack_keys_body,
        out_shape=[
            jax.ShapeDtypeStruct((2 * tokens, width), bf16),
            jax.ShapeDtypeStruct((width, tokens), bf16),
        ],
        in_specs=[whole] * 2,
        out_specs=[whole] * 2,
        compiler_params=params(),
    )(keys, values)


def columns_to_rows(columns):
    tokens = columns[0].shape[0]
    lane = lax.broadcasted_iota(jnp.int32, (tokens, 128), 1)
    table = jnp.zeros((tokens, 128), f32)
    for index, column in enumerate(columns):
        table = jnp.where(lane == index, column, table)
    return table.T[:8]


def fields(branch, own, far):
    own_field = own[...].astype(f32)
    far_field = far[...].astype(f32)
    first = branch[0] == 0
    return (
        own_field,
        jnp.where(first, own_field, far_field),
        jnp.where(first, far_field, own_field),
    )


def token_sums_body(branch, own, far, target, sums):
    _, cond, uncond = fields(branch, own, far)
    teacher = target[...].astype(f32)
    sums[...] = columns_to_rows(
        [
            jnp.sum(uncond * uncond, axis=1, keepdims=True),
            jnp.sum(cond * uncond, axis=1, keepdims=True),
            jnp.sum(teacher * uncond, axis=1, keepdims=True),
        ]
    )


def token_sums(branch, own, far, target):
    return pl.pallas_call(
        token_sums_body,
        out_shape=jax.ShapeDtypeStruct((8, own.shape[0]), f32),
        in_specs=[pl.BlockSpec(memory_space=pltpu.SMEM)] + [whole] * 3,
        out_specs=whole,
        compiler_params=params(),
    )(branch, own, far, target)


def output_grads_body(branch, own, far, target, sums_a, sums_b, packed):
    tokens = own.shape[0]
    own_field, cond, uncond = fields(branch, own, far)
    teacher = target[...].astype(f32)
    total = sums_a[...] + sums_b[...]
    table = jnp.concatenate([total, jnp.zeros((120, tokens), f32)], axis=0).T
    square_sum = table[:, 0:1]
    cross_sum = table[:, 1:2]
    teacher_sum = table[:, 2:3]
    denominator = square_sum + epsilon
    projection = cross_sum / denominator
    projected = projection * uncond
    guided = projected + guide_scale * (cond - projected)
    residual = guided - teacher
    along = (
        guide_scale * cross_sum + (1.0 - guide_scale) * projection * square_sum - teacher_sum
    )
    pull = (1.0 - guide_scale) * along / denominator
    grad_cond = guide_scale * residual + pull * uncond
    grad_uncond = (1.0 - guide_scale) * projection * residual + pull * (cond - 2.0 * projected)
    douts = jnp.where(branch[0] == 0, grad_cond, grad_uncond).astype(bf16)
    packed[:tokens, :] = douts
    products = douts.astype(f32) * own_field
    deltas = columns_to_rows(
        [jnp.sum(products[:, h * 128 : h * 128 + 128], axis=1, keepdims=True) for h in range(2)]
    )
    packed[tokens:, :] = split_rows(deltas[:2])


def output_grads(branch, own, far, target, sums):
    tokens, width = own.shape
    return pl.pallas_call(
        output_grads_body,
        out_shape=jax.ShapeDtypeStruct((tokens + extra_rows, width), bf16),
        in_specs=[pl.BlockSpec(memory_space=pltpu.SMEM)] + [whole] * 5,
        out_specs=whole,
        compiler_params=params(),
    )(branch, own, far, target, *sums)


def attention_body(units, counts, modes, *refs):
    turn, started, ends, partial = modes
    takes = []
    for count in counts:
        takes.append(refs[:count])
        refs = refs[count:]
    queries, grads, blocks, turned, starts, terms = takes
    tokens = blocks[0].shape[0] // 2
    dq_out, refs = refs[: len(units)], refs[len(units) :]
    if turn:
        turned, refs = refs[: len(blocks)], refs[len(blocks) :]
        for both, across in zip(blocks, turned, strict=True):
            across[...] = both[:tokens, :].T
    scratch = list(refs[len(blocks) :])
    results = refs[: len(blocks)]
    totals = [r if end is None else scratch.pop(0) for r, end in zip(results, ends, strict=True)]
    seen = set()
    for unit, (query_at, query_lane, grad_at, grad_lane, head) in enumerate(units):
        feature = slice(head * 128, head * 128 + 128)
        query = queries[query_at][:tokens, query_lane : query_lane + 128]
        grad = grads[grad_at][:tokens, grad_lane : grad_lane + 128]
        log_row = joined_row(queries[query_at], tokens, query_lane)
        delta_row = joined_row(grads[grad_at], tokens, grad_lane)
        turned_dq = None
        for block, both in enumerate(blocks):
            total = totals[block]
            key = both[:tokens, feature]
            value = both[tokens:, feature]
            scores = lax.dot_general(key, query, both_last, preferred_element_type=f32)
            weights = jnp.exp2(scores * (score_scale * log2e) - log_row)
            dweights = lax.dot_general(value, grad, both_last, preferred_element_type=f32)
            dscores = (weights * (dweights - delta_row)).astype(bf16)
            dv_term = jnp.dot(weights.astype(bf16), grad, preferred_element_type=f32)
            dk_term = jnp.dot(dscores, query, preferred_element_type=f32)
            if head in seen:
                total[tokens:, feature] += dv_term
                total[:tokens, feature] += dk_term
            elif started:
                total[tokens:, feature] = starts[block][tokens:, feature] + dv_term
                total[:tokens, feature] = starts[block][:tokens, feature] + dk_term
            else:
                total[tokens:, feature] = dv_term
                total[:tokens, feature] = dk_term
            term = jnp.dot(turned[block][feature, :], dscores, preferred_element_type=f32)
            turned_dq = term if turned_dq is None else turned_dq + term
        seen.add(head)
        dq = turned_dq.T * score_scale
        if partial:
            dq = dq + terms[unit][...]
        dq_out[unit][...] = dq.astype(dq_out[unit].dtype)
    for done, total, end in zip(results, totals, ends, strict=True):
        if end is not None:
            done[:tokens, :] = (total[:tokens, :] * score_scale).astype(end)
            done[tokens:, :] = total[tokens:, :].astype(end)


def attention(units, queries, grads, blocks, turned, totals, out_types, ends=None, terms=()):
    tokens = blocks[0].shape[0] // 2
    groups = (queries, grads, blocks, turned, totals, terms)
    operands = [x for group in groups for x in group]
    ends = ends or [None] * len(blocks)
    turn = not turned
    outs = [jax.ShapeDtypeStruct((tokens, 128), t) for t in out_types]
    if turn:
        outs += [jax.ShapeDtypeStruct((256, tokens), bf16)] * len(blocks)
    at = len(operands) - len(terms) - len(totals)
    aliases = {
        at + i: len(outs) + i for i in range(len(totals)) if ends[i] is None
    }
    outs += [jax.ShapeDtypeStruct((2 * tokens, 256), end or f32) for end in ends]
    scratch = [pltpu.VMEM((2 * tokens, 256), f32) for end in ends if end is not None]
    products = len(units) * 5 * tokens * len(blocks) * tokens * 128
    result = pl.pallas_call(
        functools.partial(
            attention_body,
            units,
            [len(g) for g in groups],
            (turn, bool(totals), ends, bool(terms)),
        ),
        out_shape=outs,
        in_specs=[whole] * len(operands),
        out_specs=[whole] * len(outs),
        scratch_shapes=scratch,
        input_output_aliases=aliases,
        compiler_params=params(),
        cost_estimate=pl.CostEstimate(
            flops=4 * products, bytes_accessed=4 * 1024 * 1024, transcendentals=0
        ),
    )(*operands)
    return result[: len(units)], result[len(units) :]


def finish_body(total, done):
    tokens = total.shape[0] // 2
    done[:tokens, :] = total[:tokens, :] * score_scale
    done[tokens:, :] = total[tokens:, :]


def finish(total):
    return pl.pallas_call(
        finish_body,
        out_shape=jax.ShapeDtypeStruct(total.shape, f32),
        in_specs=[whole],
        out_specs=whole,
        compiler_params=params(),
        cost_estimate=pl.CostEstimate(
            flops=2 * 10**9, bytes_accessed=2 * total.size * 4, transcendentals=0
        ),
    )(total)


def shift(x, by):
    peers = lax.axis_size("ring")
    return lax.ppermute(x, "ring", [(i, (i + by) % peers) for i in range(peers)])


def swap(x, axis):
    return lax.ppermute(x, axis, [(0, 1), (1, 0)])


def local(queries, keys, values, outputs, log_sums, target):
    tokens = keys.shape[1]
    own = outputs[0]
    far = swap(own, "cfg")
    query_block = pack_queries(queries[0], log_sums[0])
    branch = lax.axis_index("cfg").astype(jnp.int32).reshape(1)
    query_block, own_keys, own_values = lax.optimization_barrier(
        (query_block, keys[0], values[0])
    )
    own_block, own_turned = pack_keys(own_keys, own_values)
    far_block = swap(own_block, "pair")
    q1 = (shift(query_block, 1), shift(query_block, -1))
    sums = token_sums(branch, own, far, target)
    sums = sums + swap(sums, "core")
    sums_near = lax.ppermute(sums, "x", [(i, i ^ 1) for i in range(4)])
    sums_near, q1 = lax.optimization_barrier((sums_near, q1))
    sums = sums + sums_near
    sums_far = lax.ppermute(sums, "x", [(i, 3 - i) for i in range(4)])
    q2 = (shift(q1[0], 1), shift(q1[1], -1))
    grad_block = output_grads(branch, own, far, target, [sums, sums_far])
    d1 = (shift(grad_block, 1), shift(grad_block, -1))
    q3 = (shift(q2[0], 1), shift(q2[1], -1))
    d2 = (shift(d1[0], 1), shift(d1[1], -1))

    blocks = [own_block, far_block]
    pair_units = (
        (0, 0, 0, 0, 0),
        (0, 128, 0, 128, 1),
        (1, 0, 1, 0, 0),
        (1, 128, 1, 128, 1),
    )
    near_units = pair_units + ((2, 0, 2, 0, 0), (2, 128, 2, 128, 1))
    last_units = ((0, 256, 0, 0, 0), (1, 256, 1, 0, 1))
    near = (near_units, (*q1, query_block), (*d1, grad_block))
    near_terms, (far_turned, far_total) = attention(*near, blocks[1:], (), (), [f32] * 6)
    d2, near_terms = lax.optimization_barrier((d2, near_terms))
    ahead = (
        jnp.concatenate([d2[0], q3[0][:, :128]], axis=1),
        jnp.concatenate([d2[1], q3[1][:, 128:]], axis=1),
    )
    d3 = (shift(ahead[0], 1), shift(ahead[1], -1))
    d4 = (shift(d3[0][:, :128], 1), shift(d3[1][:, 128:256], -1))
    run = functools.partial(attention, blocks=blocks, turned=(own_turned, far_turned))
    near_terms, (own_total,) = attention(
        *near, blocks[:1], (own_turned,), (), [f32] * 6, terms=near_terms
    )
    p1, p0 = near_terms[:4], near_terms[4:]
    p3, totals = run(
        pair_units, q3, d3, totals=(own_total, far_total), out_types=[bf16] * 4
    )
    p4, totals = run(last_units, d3, d4, totals=totals, out_types=[bf16] * 2)
    p2, (own_total, sent) = run(
        pair_units, q2, d2, totals=totals, out_types=[f32] * 4, ends=[None, bf16]
    )

    def home(right, left, steps=1):
        return lax.optimization_barrier((shift(right, -steps), shift(left, steps)))

    def beside(first, second):
        return jnp.concatenate([first, second], axis=1)

    def joined(first, second, arrived):
        return (beside(first, second) + arrived.astype(f32)).astype(bf16)

    a_right, a_left = home(*p4, steps=2)
    right, left = home(beside(p3[0], p3[1]), beside(p3[2], p3[3]))
    right, left, own_total = lax.optimization_barrier((right, left, own_total))
    right = joined(p2[0] + a_right.astype(f32), p2[1], right)
    left = joined(p2[2], p2[3] + a_left.astype(f32), left)
    right, left = home(right, left)
    dkv_own = finish(own_total)
    dkv_own, sent = lax.optimization_barrier((dkv_own, sent))
    dkv_far = swap(sent, "pair")
    right, left = home(joined(p1[0], p1[1], right), joined(p1[2], p1[3], left))
    dq = beside(*p0) + right.astype(f32) + left.astype(f32)
    grad_queries = dq.astype(bf16)[None]
    dkv = (dkv_own + dkv_far.astype(f32)).astype(bf16)
    return (grad_queries, dkv[:tokens][None], dkv[tokens:][None])


def solution(mesh):
    split = Mesh(
        mesh.devices.reshape(4, 2, 8, 2, 2), ("x", "core", "ring", "pair", "cfg")
    )
    rows, columns = ("ring", "pair"), ("x", "core")
    in_specs = (
        P("cfg", rows, columns),
        P("cfg", rows, columns),
        P("cfg", rows, columns),
        P("cfg", rows, columns),
        P("cfg", columns, rows),
        P(rows, columns),
    )
    out_specs = (P("cfg", rows, columns),) * 3
    return jax.shard_map(
        local, mesh=split, in_specs=in_specs, out_specs=out_specs, check_vma=False
    )
```
